32 devices in a mesh: expert: 8 (over z, y), tensor: 4 (over x, core).
Axes of the slice: x: 2, y: 2, z: 4, core: 2. Of those that a mesh axis runs over, the one named last changes fastest.
Arguments:
- hidden_in: bfloat16 [4096, 1536], P('expert', 'tensor'), may hold values from -50 to 50
- cache_lengths: int32 [8], P('expert'), may hold values from 0 to 8192, as said below
- new_lengths: int32 [8], P('expert'), may hold values from 128 to 512, as said below
- key_cache: bfloat16 [8, 8192, 256], P('expert'), may hold values from -120 to 120
- cached_value_rows: bfloat16 [8, 8192, 256], P('expert'), may hold values from -6 to 6
- attn_gain: float32 [1536], replicated, may hold values from 0.1 to 1.9
- w_query: bfloat16 [1536, 1536], P(None, 'tensor'), may hold values from -0.15625 to 0.15625
- key_matrix: bfloat16 [1536, 256], replicated, may hold values from -0.15625 to 0.15625
- value_matrix: bfloat16 [1536, 256], replicated, may hold values from -0.15625 to 0.15625
- w_out: bfloat16 [1536, 1536], P('tensor'), may hold values from -0.5 to 0.5
- moe_gain: float32 [1536], replicated, may hold values from 0.1 to 1.9
- route_ids: int32 [4096, 4], P('expert'), may hold values from 0 to 7, all different within a row; in each aligned block of 512 rows (0 to 511, 512 to 1023, ...) at most 384 rows name the same one
- route_weights: float32 [4096, 4], P('expert'), may hold values from 0.1 to 1
- w_gate: bfloat16 [8, 1536, 768], P('expert', None, 'tensor'), may hold values from -0.15625 to 0.15625
- w_up: bfloat16 [8, 1536, 768], P('expert', None, 'tensor'), may hold values from -0.15625 to 0.15625
- w_down: bfloat16 [8, 768, 1536], P('expert', 'tensor'), may hold values from -0.21875 to 0.21875
Outputs:
- mixed: bfloat16 [4096, 1536], P('expert', 'tensor')
The draws below stay inside these ranges and needn't reach their ends.
Inputs may be any that keep to these rules, and one draw needn't show every extreme that they name: `cache_lengths`: A third of the 8 requests, rounded up, hold an empty cache; at least one holds 8192 positions. `new_lengths`: at least one request has all 512 new tokens valid. `route_ids`: each row names 4 different experts. Within the 512 rows of one request no expert is named by more than 384 rows, and in some request some expert is named by exactly 384 rows.
All inputs are finite; a program needn't handle non-finite values.
Results may differ from the reference program's by a relative error of at most 0.013.
Values may be sent and summed in bfloat16 or wider, within the bound.
A program may use at most 192 MiB of HBM per device.

```python
import math
import jax
import jax.numpy as jnp
import numpy as np
from jax import lax

MODEL_DIM = 1536
QUERY_HEADS = 12
KEY_VALUE_HEADS = 2
HEAD_DIM = 128
FF_E = 768
TOP = 4
NEW_TOK = 512
CACHE_LIMIT = 8192
EXPERTS = 8
REQUEST_COUNT = 8
TOKENS = 4096
CAP = 384
N_EXPERT = 8
N_TENSOR = 4


def draw_hidden_in(key, part):
    base_key, row_key, column_key = jax.random.split(key, 3)
    row_scale = jnp.exp(jax.random.uniform(row_key, (TOKENS, 1), jnp.float32, math.log(0.3), math.log(3.0)))
    column_scale = jnp.exp(jax.random.uniform(column_key, (1, MODEL_DIM), jnp.float32, math.log(0.3), math.log(3.0)))
    values = jnp.clip(jax.random.normal(base_key, (TOKENS, MODEL_DIM), jnp.float32), -5.0, 5.0) * row_scale * column_scale
    return values.astype(jnp.bfloat16)


def draw_key_cache(key, part):
    base_key = jax.random.fold_in(jax.random.fold_in(key, 41), 0)
    key_value_width = KEY_VALUE_HEADS * HEAD_DIM
    values = jnp.clip(jax.random.normal(base_key, (REQUEST_COUNT, CACHE_LIMIT, key_value_width), jnp.float32), -5.0, 5.0)
    return values.astype(jnp.bfloat16)


def draw_cache_lengths(key, part):
    length_key, order_key = jax.random.split(jax.random.fold_in(key, 17))
    lengths = jax.random.randint(length_key, (REQUEST_COUNT,), 1, CACHE_LIMIT + 1, dtype=jnp.int32)
    ranking = jax.random.permutation(order_key, REQUEST_COUNT).astype(jnp.int32)
    lengths = jnp.where(ranking % 3 == 0, 0, lengths)
    lengths = jnp.where(ranking == 1, CACHE_LIMIT, lengths)
    return lengths.astype(jnp.int32)


def draw_new_lengths(key, part):
    length_key, order_key = jax.random.split(jax.random.fold_in(key, 29))
    lengths = jax.random.randint(length_key, (REQUEST_COUNT,), NEW_TOK // 4, NEW_TOK + 1, dtype=jnp.int32)
    ranking = jax.random.permutation(order_key, REQUEST_COUNT).astype(jnp.int32)
    lengths = jnp.where(ranking == 0, NEW_TOK, lengths)
    return lengths.astype(jnp.int32)


def block_levels(rng, dims, cuts, least, high):
    factor_of, own = 1.0, jax.random.fold_in(rng, 6)
    for dim, parts in cuts:
        draws = jnp.exp(jax.random.uniform(jax.random.fold_in(own, dim), (parts,), jnp.float32, least / len(cuts), high / len(cuts)))
        factor_of = factor_of * jnp.repeat(draws, dims[dim] // parts).reshape([-1 if axis == dim else 1 for axis in range(len(dims))])
    return factor_of


def assign_block(stream_key, own, number, rows, amount, top, most, skew):
    sequence = jax.random.permutation(stream_key, amount)
    packed, ordinary = load_shares(amount, rows * top, most, skew, True), load_shares(amount, rows * top, most, skew, False)
    places = jnp.arange(amount)

    def named(tallies, offset_by):
        used = int((tallies > 0).sum())
        fixed = max(1, used // 4)
        passed = fixed + (places - fixed + offset_by * (used - fixed)) % max(1, amount - fixed)
        return jnp.zeros((amount,), jnp.int32).at[sequence[jnp.where(places < fixed, places, passed)]].set(jnp.asarray(tallies, jnp.int32))

    tallies = jnp.where(number % 4 == 0, named(packed, number // 4), named(ordinary, number - number // 4 - 1))
    mixed = jax.random.permutation(jax.random.fold_in(own, 3), amount)
    giver, receiver = mixed[0:amount // 2 * 2:2], mixed[1:amount // 2 * 2:2]
    slack = jnp.minimum(tallies[giver] - 1, most - tallies[receiver]) // 2
    slack = jnp.where((giver == sequence[0]) | (receiver == sequence[0]) | (tallies[receiver] == 0), 0, jnp.maximum(slack, 0))
    passed = jax.random.randint(jax.random.fold_in(own, 4), (amount // 2,), 0, 1 << 20) % (slack + 1)
    tallies = tallies.at[giver].add(-passed).at[receiver].add(passed)
    members = jnp.searchsorted(jnp.cumsum(tallies), jnp.arange(rows * top), side="right").astype(jnp.int32)
    listing = members.reshape(top, rows).T
    listing = listing[jax.random.permutation(jax.random.fold_in(own, 1), rows)]
    offset_by = jax.random.randint(jax.random.fold_in(own, 2), (rows, 1), 0, top)
    return jnp.take_along_axis(listing, (jnp.arange(top)[None, :] + offset_by) % top, axis=1)


def load_shares(number_of, total, limit, skew, full):
    weights = [(1 << 20) // math.isqrt(grade ** skew) + 1 for grade in range(1, number_of + 1)]
    largest = limit if full else min(limit, max(-(-total // number_of), total * weights[0] // sum(weights)))
    least = 1 if total - largest >= number_of - 1 else 0
    holding, spare = [largest] + [least] * (number_of - 1), total - largest - least * (number_of - 1)
    while spare > 0:
        candidates = [i for i in range(1, number_of) if holding[i] < largest] or [i for i in range(1, number_of) if holding[i] < limit]
        mass, left = sum([weights[i] for i in candidates]), spare
        for i in candidates:
            extra = min(limit - holding[i], max(1, left * weights[i] // mass), spare)
            holding[i] = holding[i] + extra
            spare = spare - extra
    return np.array(holding)


def normal_values(rng, shape, spread, reach, cuts=(), held_as=jnp.bfloat16):
    values = jax.random.normal(rng, shape, jnp.float32) * spread
    if len(cuts) > 0:
        values = block_levels(rng, shape, cuts, -0.22, 0.18) * values
    return jnp.clip(values, min=-reach, max=reach).astype(held_as)


def setup_inputs(seed: int = 0) -> dict:
    streams_of = jax.random.split(jax.random.key(seed), 17)
    hidden_in = draw_hidden_in(jax.random.fold_in(streams_of[16], 71), 0)
    cache_lengths = draw_cache_lengths(jax.random.fold_in(streams_of[16], 71), 0)
    new_lengths = draw_new_lengths(jax.random.fold_in(streams_of[16], 71), 0)
    key_cache = draw_key_cache(jax.random.fold_in(streams_of[16], 71), 0)
    cached_value_rows = normal_values(streams_of[4], (REQUEST_COUNT, CACHE_LIMIT, KEY_VALUE_HEADS * HEAD_DIM), 1.0, 6.0, ((0, 8),))
    attn_gain = jnp.clip(1.0 + 0.18 * jax.random.normal(streams_of[5], (MODEL_DIM,), jnp.float32), 0.1, 1.9)
    w_query = normal_values(streams_of[6], (MODEL_DIM, QUERY_HEADS * HEAD_DIM), MODEL_DIM ** -0.5, 0.15625, ((1, 4),))
    key_matrix = normal_values(streams_of[7], (MODEL_DIM, KEY_VALUE_HEADS * HEAD_DIM), MODEL_DIM ** -0.5, 0.15625)
    value_matrix = normal_values(streams_of[8], (MODEL_DIM, KEY_VALUE_HEADS * HEAD_DIM), MODEL_DIM ** -0.5, 0.15625)
    w_out = normal_values(streams_of[9], (QUERY_HEADS * HEAD_DIM, MODEL_DIM), HEAD_DIM ** -0.5, 0.5, ((0, 4),))
    moe_gain = jnp.clip(1.0 + 0.18 * jax.random.normal(streams_of[10], (MODEL_DIM,), jnp.float32), 0.1, 1.9)
    route_ids_keys = jax.random.split(jax.random.fold_in(streams_of[11], 1), TOKENS // NEW_TOK)
    route_ids_turns = jax.random.permutation(jax.random.fold_in(streams_of[11], 3), TOKENS // NEW_TOK)
    route_ids = jax.vmap(lambda own, number: assign_block(jax.random.fold_in(streams_of[11], 2), own, number, NEW_TOK, EXPERTS, TOP, CAP, 2))(route_ids_keys, route_ids_turns).reshape((TOKENS, TOP))
    route_weights = jnp.clip(jnp.exp(math.log(1.0) - 2.3025851 * jax.random.uniform(streams_of[12], (TOKENS, TOP), jnp.float32) ** block_levels(streams_of[12], (TOKENS, TOP), ((0, 8),), -0.2, 0.2)), 0.1, 1.0)
    w_gate = normal_values(streams_of[13], (EXPERTS, MODEL_DIM, FF_E), MODEL_DIM ** -0.5, 0.15625, ((0, 8), (2, 4)))
    w_up = normal_values(streams_of[14], (EXPERTS, MODEL_DIM, FF_E), MODEL_DIM ** -0.5, 0.15625, ((0, 8), (2, 4)))
    w_down = normal_values(streams_of[15], (EXPERTS, FF_E, MODEL_DIM), FF_E ** -0.5, 0.21875, ((0, 8), (1, 4)))
    return {"hidden_in": hidden_in, "cache_lengths": cache_lengths, "new_lengths": new_lengths, "key_cache": key_cache, "cached_value_rows": cached_value_rows, "attn_gain": attn_gain, "w_query": w_query, "key_matrix": key_matrix, "value_matrix": value_matrix, "w_out": w_out, "moe_gain": moe_gain, "route_ids": route_ids, "route_weights": route_weights, "w_gate": w_gate, "w_up": w_up, "w_down": w_down}


epsilon = 1e-06
contract = (((1,), (1,)), ((), ()))

def norm_rows(activity, gain_vector):
    values = activity.astype(jnp.float32)
    mean_square = lax.optimization_barrier(jnp.mean(values * values, axis=-1, keepdims=True))
    return (values * lax.rsqrt(mean_square + epsilon) * gain_vector).astype(jnp.bfloat16)

def fresh_scores(query_rows, new_keys, new_length, scaling):
    scores = lax.dot_general(query_rows, new_keys, contract, preferred_element_type=jnp.float32) * scaling
    query_place = jnp.arange(query_rows.shape[0], dtype=jnp.int32)
    key_place = jnp.arange(new_keys.shape[0], dtype=jnp.int32)
    allowed = (key_place[None, :] <= query_place[:, None]) & (key_place[None, :] < new_length)
    return jnp.where(allowed, scores, -jnp.inf)

def attend(query_rows, past_keys, past_values, cache_length, new_keys, new_values, new_length):
    scaling = 1.0 / math.sqrt(query_rows.shape[1])
    cache_scores = lax.dot_general(query_rows, past_keys, contract, preferred_element_type=jnp.float32) * scaling
    cache_place = jnp.arange(past_keys.shape[0], dtype=jnp.int32)
    cache_scores = jnp.where(cache_place[None, :] < cache_length, cache_scores, -jnp.inf)
    new_scores = fresh_scores(query_rows, new_keys, new_length, scaling)
    row_max = jnp.maximum(lax.optimization_barrier(jnp.max(cache_scores, axis=1)), lax.optimization_barrier(jnp.max(new_scores, axis=1)))
    cache_weight = jnp.exp(cache_scores - row_max[:, None])
    new_weight = jnp.exp(new_scores - row_max[:, None])
    denominator = lax.optimization_barrier(jnp.sum(cache_weight, axis=1)) + lax.optimization_barrier(jnp.sum(new_weight, axis=1))
    summed = jnp.dot(cache_weight.astype(jnp.bfloat16), past_values, preferred_element_type=jnp.float32)
    summed = summed + jnp.dot(new_weight.astype(jnp.bfloat16), new_values, preferred_element_type=jnp.float32)
    return (summed / denominator[:, None]).astype(jnp.bfloat16)

def reference(hidden_in, cache_lengths, new_lengths, key_cache, cached_value_rows, attn_gain, w_query, key_matrix, value_matrix, w_out, moe_gain, route_ids, route_weights, w_gate, w_up, w_down):
    attn_in = norm_rows(hidden_in, attn_gain)
    queries = jnp.dot(attn_in, w_query, preferred_element_type=jnp.float32).astype(jnp.bfloat16)
    new_keys = jnp.dot(attn_in, key_matrix, preferred_element_type=jnp.float32).astype(jnp.bfloat16)
    new_values = jnp.dot(attn_in, value_matrix, preferred_element_type=jnp.float32).astype(jnp.bfloat16)
    query_group_count = QUERY_HEADS // KEY_VALUE_HEADS

    def one_request(request):
        row_start = request * NEW_TOK
        query_block = lax.dynamic_slice_in_dim(queries, row_start, NEW_TOK, 0)
        key_block = lax.dynamic_slice_in_dim(new_keys, row_start, NEW_TOK, 0)
        value_block = lax.dynamic_slice_in_dim(new_values, row_start, NEW_TOK, 0)
        past_keys = key_cache[request]
        past_values = cached_value_rows[request]
        cache_length = cache_lengths[request]
        new_length = new_lengths[request]
        heads_out = []
        for head_index in range(QUERY_HEADS):
            shared = head_index // query_group_count
            heads_out.append(attend(query_block[:, head_index * HEAD_DIM:(head_index + 1) * HEAD_DIM], past_keys[:, shared * HEAD_DIM:(shared + 1) * HEAD_DIM], past_values[:, shared * HEAD_DIM:(shared + 1) * HEAD_DIM], cache_length, key_block[:, shared * HEAD_DIM:(shared + 1) * HEAD_DIM], value_block[:, shared * HEAD_DIM:(shared + 1) * HEAD_DIM], new_length))
        return jnp.concatenate(heads_out, axis=1)
    context = lax.map(one_request, jnp.arange(REQUEST_COUNT, dtype=jnp.int32)).reshape(TOKENS, QUERY_HEADS * HEAD_DIM)
    residual = (hidden_in.astype(jnp.float32) + jnp.dot(context, w_out, preferred_element_type=jnp.float32)).astype(jnp.bfloat16)
    moe_in = norm_rows(residual, moe_gain)
    flat_ids = route_ids.reshape(-1).astype(jnp.int32)
    sorted_slots = jnp.argsort(flat_ids, stable=True).astype(jnp.int32)
    one_hot = (flat_ids[:, None] == jnp.arange(EXPERTS, dtype=jnp.int32)[None, :]).astype(jnp.int32)
    counts = lax.optimization_barrier(jnp.sum(one_hot, axis=0)).astype(jnp.int32)
    starts = (jnp.cumsum(counts) - counts).astype(jnp.int32)
    capacity = CAP * N_EXPERT
    padded_order = jnp.concatenate([sorted_slots, jnp.zeros((capacity,), jnp.int32)])
    quarter = FF_E // N_TENSOR

    def one_expert(outputs, expert):
        picked_slots = lax.dynamic_slice_in_dim(padded_order, starts[expert], capacity, 0)
        valid_slot = jnp.arange(capacity, dtype=jnp.int32) < counts[expert]
        inputs = moe_in[picked_slots // TOP]
        gate_value = jnp.dot(inputs, w_gate[expert], preferred_element_type=jnp.float32)
        upward = jnp.dot(inputs, w_up[expert], preferred_element_type=jnp.float32)
        active = (jnp.maximum(gate_value, 0.0) * upward).astype(jnp.bfloat16)
        combined = jnp.zeros((capacity, MODEL_DIM), jnp.float32)
        for quarter_index in range(N_TENSOR):
            partial_sum = jnp.dot(active[:, quarter_index * quarter:(quarter_index + 1) * quarter], w_down[expert, quarter_index * quarter:(quarter_index + 1) * quarter], preferred_element_type=jnp.float32)
            combined = combined + lax.optimization_barrier(partial_sum.astype(jnp.bfloat16)).astype(jnp.float32)
        result = jnp.where(valid_slot[:, None], combined.astype(jnp.bfloat16), jnp.zeros((), jnp.bfloat16))
        return (outputs.at[picked_slots].add(result), None)
    expert_out, unused = lax.scan(one_expert, jnp.zeros((TOKENS * TOP, MODEL_DIM), jnp.bfloat16), jnp.arange(EXPERTS, dtype=jnp.int32))
    expert_out = expert_out.reshape(TOKENS, TOP, MODEL_DIM)
    mixed_rows = residual.astype(jnp.float32)
    for slot_index in range(TOP):
        mixed_rows = mixed_rows + route_weights[:, slot_index, None] * expert_out[:, slot_index].astype(jnp.float32)
    return mixed_rows.astype(jnp.bfloat16)
```

```python
import functools
import math

import jax
import jax.numpy as jnp
from jax import lax
from jax.experimental import pallas as pl
from jax.experimental.pallas import tpu as pltpu
from jax.sharding import PartitionSpec as P

QUERY_HEADS = 12
KEY_VALUE_HEADS = 2
HEAD_DIM = 128
TOP = 4
BLOCK = 1024

epsilon = 1e-06


def norm_rows(activity, gain_vector):
    values = activity.astype(jnp.float32)
    mean_square = jnp.mean(values * values, axis=-1, keepdims=True)
    return (values * lax.rsqrt(mean_square + epsilon) * gain_vector).astype(jnp.bfloat16)


def attention_kernel(
    heads, scale, info, q_ref, nk_ref, nv_ref, k_ref, v_ref, out_ref, top, total, acc
):
    step = pl.program_id(0)
    length = info[0]
    fresh = info[1]
    block = k_ref.shape[1]
    rows = q_ref.shape[1]

    def visit(head, keys, values, mask, first):
        scores = jnp.dot(
            keys,
            q_ref[head * HEAD_DIM : (head + 1) * HEAD_DIM, :],
            preferred_element_type=jnp.float32,
        )
        if mask is not None:
            scores = jnp.where(mask, scores, -jnp.inf)
        largest = jnp.max(scores, axis=0, keepdims=True)
        if not first:
            before = top[head : head + 1, :]
            largest = jnp.maximum(largest, before)
        weights = jnp.exp2((scores - largest) * scale)
        added = jnp.sum(weights, axis=0, keepdims=True)
        product = lax.dot_general(
            values,
            weights.astype(jnp.bfloat16),
            (((0,), (0,)), ((), ())),
            preferred_element_type=jnp.float32,
        )
        if not first:
            alpha = jnp.exp2((before - largest) * scale)
            added = added + total[head : head + 1, :] * alpha
            product = product + acc[head] * alpha
        top[head : head + 1, :] = largest
        total[head : head + 1, :] = added
        acc[head] = product

    @pl.when(step == 0)
    def _():
        count = nk_ref.shape[0]
        key_place = lax.broadcasted_iota(jnp.int32, (count, rows), 0)
        query_place = lax.broadcasted_iota(jnp.int32, (count, rows), 1)
        mask = (key_place <= query_place) & (key_place < fresh)
        for head in range(heads):
            visit(head, nk_ref[...], nv_ref[...], mask, True)

    start = (step - 1) * block

    @pl.when((step > 0) & (start + block <= length))
    def _():
        for head in range(heads):
            visit(head, k_ref[0], v_ref[0], None, False)

    @pl.when((step > 0) & (start < length) & (start + block > length))
    def _():
        place = lax.broadcasted_iota(jnp.int32, (block, rows), 0) + start
        for head in range(heads):
            visit(head, k_ref[0], v_ref[0], place < length, False)

    @pl.when(step == pl.num_programs(0) - 1)
    def _():
        for head in range(heads):
            result = acc[head] / total[head : head + 1, :]
            out_ref[:, head * HEAD_DIM : (head + 1) * HEAD_DIM] = result.T.astype(jnp.bfloat16)


def attention(queries_t, new_keys, new_values, keys, values, length, fresh, shared):
    heads = queries_t.shape[0] // HEAD_DIM
    rows = queries_t.shape[1]
    limit = keys.shape[1]
    block = min(BLOCK, limit)
    scale = math.log2(math.e) / math.sqrt(HEAD_DIM)
    info = jnp.stack([length, fresh, shared]).astype(jnp.int32)

    def place(step, info):
        last = jnp.maximum((info[0] + block - 1) // block - 1, 0)
        return (0, jnp.minimum(jnp.maximum(step - 1, 0), last), info[2])

    return pl.pallas_call(
        functools.partial(attention_kernel, heads, scale),
        grid_spec=pltpu.PrefetchScalarGridSpec(
            num_scalar_prefetch=1,
            grid=(1 + limit // block,),
            in_specs=[
                pl.BlockSpec(queries_t.shape, lambda step, info: (0, 0)),
                pl.BlockSpec(new_keys.shape, lambda step, info: (0, 0)),
                pl.BlockSpec(new_values.shape, lambda step, info: (0, 0)),
                pl.BlockSpec((1, block, HEAD_DIM), place),
                pl.BlockSpec((1, block, HEAD_DIM), place),
            ],
            out_specs=pl.BlockSpec((rows, heads * HEAD_DIM), lambda step, info: (0, 0)),
            scratch_shapes=[
                pltpu.VMEM((8, rows), jnp.float32),
                pltpu.VMEM((8, rows), jnp.float32),
                pltpu.VMEM((heads, HEAD_DIM, rows), jnp.float32),
            ],
        ),
        out_shape=jax.ShapeDtypeStruct((rows, heads * HEAD_DIM), jnp.bfloat16),
        compiler_params=pltpu.CompilerParams(vmem_limit_bytes=40 * 1024 * 1024),
        cost_estimate=pl.CostEstimate(
            flops=4 * heads * rows * limit * HEAD_DIM,
            bytes_accessed=4 * limit * HEAD_DIM,
            transcendentals=heads * rows * limit,
        ),
        name="attention",
    )(info, queries_t, new_keys, new_values, keys, values)


def local(
    hidden_in,
    cache_lengths,
    new_lengths,
    key_cache,
    cached_value_rows,
    attn_gain,
    w_query,
    key_matrix,
    value_matrix,
    w_out,
    moe_gain,
    route_ids,
    route_weights,
    w_gate,
    w_up,
    w_down,
):
    tensor_count = lax.axis_size("tensor")
    tensor_index = lax.axis_index("tensor")
    expert_index = lax.axis_index("expert")
    new_count = hidden_in.shape[0]
    quarter = new_count // tensor_count
    local_heads = w_query.shape[1] // HEAD_DIM
    query_group_count = QUERY_HEADS // KEY_VALUE_HEADS
    shared = tensor_index * local_heads // query_group_count
    expert_total = w_gate.shape[0] * lax.axis_size("expert")

    full_rows = lax.all_gather(hidden_in, "tensor", axis=1, tiled=True)
    whole_out = lax.all_gather(w_out, "tensor", axis=0, tiled=True)
    whole_gate = lax.all_gather(w_gate[0], "tensor", axis=0, tiled=False)
    whole_up = lax.all_gather(w_up[0], "tensor", axis=0, tiled=False)
    whole_down = lax.all_gather(w_down[0], "tensor", axis=0, tiled=True)

    my_ids = lax.dynamic_slice_in_dim(route_ids, tensor_index * quarter, quarter, 0)
    my_weights = lax.dynamic_slice_in_dim(route_weights, tensor_index * quarter, quarter, 0)
    named = my_ids[:, :, None] == jnp.arange(expert_total, dtype=jnp.int32)[None, None, :]
    table = jnp.sum(jnp.where(named, my_weights[:, :, None], 0.0), axis=1)
    tables = lax.all_gather(table, "expert", axis=0, tiled=True)
    row_weight = lax.dynamic_slice_in_dim(tables, expert_index, 1, 1)

    attn_in = norm_rows(full_rows, attn_gain)
    queries_t = lax.dot_general(
        w_query, attn_in, (((0,), (1,)), ((), ())), preferred_element_type=jnp.float32
    ).astype(jnp.bfloat16)
    key_weight = lax.dynamic_slice_in_dim(key_matrix, shared * HEAD_DIM, HEAD_DIM, 1)
    value_weight = lax.dynamic_slice_in_dim(value_matrix, shared * HEAD_DIM, HEAD_DIM, 1)
    both = jnp.dot(
        attn_in,
        jnp.concatenate([key_weight, value_weight], axis=1),
        preferred_element_type=jnp.float32,
    ).astype(jnp.bfloat16)
    context = attention(
        queries_t,
        both[:, :HEAD_DIM],
        both[:, HEAD_DIM:],
        key_cache,
        cached_value_rows,
        cache_lengths[0],
        new_lengths[0],
        shared,
    )
    my_context = lax.all_to_all(context, "tensor", split_axis=0, concat_axis=1, tiled=True)
    my_rows = lax.dynamic_slice_in_dim(full_rows, tensor_index * quarter, quarter, 0)
    residual = (
        my_rows.astype(jnp.float32)
        + jnp.dot(my_context, whole_out, preferred_element_type=jnp.float32)
    ).astype(jnp.bfloat16)
    moe_rows = norm_rows(residual, moe_gain)
    all_rows = lax.all_gather(moe_rows, "expert", axis=0, tiled=True)
    partial = jnp.zeros((all_rows.shape[0], all_rows.shape[1]), jnp.float32)
    actives = []
    for part in range(tensor_count):
        gate_value = jnp.dot(all_rows, whole_gate[part], preferred_element_type=jnp.float32)
        upward = jnp.dot(all_rows, whole_up[part], preferred_element_type=jnp.float32)
        actives.append((jnp.maximum(gate_value, 0.0) * upward).astype(jnp.bfloat16))
    active = jnp.concatenate(actives, axis=1)
    partial = jnp.dot(active, whole_down, preferred_element_type=jnp.float32)
    weighted = jnp.where(row_weight > 0.0, partial * row_weight, 0.0).astype(jnp.bfloat16)
    summed = lax.psum_scatter(weighted, "expert", scatter_dimension=0, tiled=True)
    mixed = (residual.astype(jnp.float32) + summed.astype(jnp.float32)).astype(jnp.bfloat16)
    return lax.all_to_all(mixed, "tensor", split_axis=1, concat_axis=0, tiled=True)


def solution(mesh):
    placed = (
        P("expert", "tensor"),
        P("expert"),
        P("expert"),
        P("expert", None, None),
        P("expert", None, None),
        P(),
        P(None, "tensor"),
        P(),
        P(),
        P("tensor", None),
        P(),
        P("expert", None),
        P("expert", None),
        P("expert", None, "tensor"),
        P("expert", None, "tensor"),
        P("expert", "tensor", None),
    )
    return jax.shard_map(
        local, mesh=mesh, in_specs=placed, out_specs=P("expert", "tensor"), check_vma=False
    )
```

```python
import functools
import math

import jax
import jax.numpy as jnp
from jax import lax
from jax.experimental import pallas as pl
from jax.experimental.pallas import tpu as pltpu
from jax.sharding import PartitionSpec as P

QUERY_HEADS = 12
KEY_VALUE_HEADS = 2
HEAD_DIM = 128
TOP = 4
BLOCK = 1024

epsilon = 1e-06


def norm_rows(activity, gain_vector):
    values = activity.astype(jnp.float32)
    mean_square = jnp.mean(values * values, axis=-1, keepdims=True)
    return (values * lax.rsqrt(mean_square + epsilon) * gain_vector).astype(jnp.bfloat16)


def attention_kernel(
    heads, scale, info, q_ref, nk_ref, nv_ref, k_ref, v_ref, out_ref, top, total, acc
):
    step = pl.program_id(0)
    length = info[0]
    fresh = info[1]
    block = k_ref.shape[1]
    rows = q_ref.shape[1]

    def visit(head, keys, values, mask, first):
        scores = jnp.dot(
            keys,
            q_ref[head * HEAD_DIM : (head + 1) * HEAD_DIM, :],
            preferred_element_type=jnp.float32,
        )
        if mask is not None:
            scores = jnp.where(mask, scores, -jnp.inf)
        largest = jnp.max(scores, axis=0, keepdims=True)
        if not first:
            before = top[head : head + 1, :]
            largest = jnp.maximum(largest, before)
        weights = jnp.exp2((scores - largest) * scale)
        added = jnp.sum(weights, axis=0, keepdims=True)
        product = lax.dot_general(
            values,
            weights.astype(jnp.bfloat16),
            (((0,), (0,)), ((), ())),
            preferred_element_type=jnp.float32,
        )
        if not first:
            alpha = jnp.exp2((before - largest) * scale)
            added = added + total[head : head + 1, :] * alpha
            product = product + acc[head] * alpha
        top[head : head + 1, :] = largest
        total[head : head + 1, :] = added
        acc[head] = product

    @pl.when(step == 0)
    def _():
        count = nk_ref.shape[0]
        key_place = lax.broadcasted_iota(jnp.int32, (count, rows), 0)
        query_place = lax.broadcasted_iota(jnp.int32, (count, rows), 1)
        mask = (key_place <= query_place) & (key_place < fresh)
        for head in range(heads):
            visit(head, nk_ref[...], nv_ref[...], mask, True)

    start = (step - 1) * block

    @pl.when((step > 0) & (start + block <= length))
    def _():
        for head in range(heads):
            visit(head, k_ref[0], v_ref[0], None, False)

    @pl.when((step > 0) & (start < length) & (start + block > length))
    def _():
        place = lax.broadcasted_iota(jnp.int32, (block, rows), 0) + start
        for head in range(heads):
            visit(head, k_ref[0], v_ref[0], place < length, False)

    @pl.when(step == pl.num_programs(0) - 1)
    def _():
        for head in range(heads):
            result = acc[head] / total[head : head + 1, :]
            out_ref[:, head * HEAD_DIM : (head + 1) * HEAD_DIM] = result.T.astype(jnp.bfloat16)


def attention(queries_t, new_keys, new_values, keys, values, length, fresh, shared):
    heads = queries_t.shape[0] // HEAD_DIM
    rows = queries_t.shape[1]
    limit = keys.shape[1]
    block = min(BLOCK, limit)
    scale = math.log2(math.e) / math.sqrt(HEAD_DIM)
    info = jnp.stack([length, fresh, shared]).astype(jnp.int32)

    def place(step, info):
        last = jnp.maximum((info[0] + block - 1) // block - 1, 0)
        return (0, jnp.minimum(jnp.maximum(step - 1, 0), last), info[2])

    return pl.pallas_call(
        functools.partial(attention_kernel, heads, scale),
        grid_spec=pltpu.PrefetchScalarGridSpec(
            num_scalar_prefetch=1,
            grid=(1 + limit // block,),
            in_specs=[
                pl.BlockSpec(queries_t.shape, lambda step, info: (0, 0)),
                pl.BlockSpec(new_keys.shape, lambda step, info: (0, 0)),
                pl.BlockSpec(new_values.shape, lambda step, info: (0, 0)),
                pl.BlockSpec((1, block, HEAD_DIM), place),
                pl.BlockSpec((1, block, HEAD_DIM), place),
            ],
            out_specs=pl.BlockSpec((rows, heads * HEAD_DIM), lambda step, info: (0, 0)),
            scratch_shapes=[
                pltpu.VMEM((8, rows), jnp.float32),
                pltpu.VMEM((8, rows), jnp.float32),
                pltpu.VMEM((heads, HEAD_DIM, rows), jnp.float32),
            ],
        ),
        out_shape=jax.ShapeDtypeStruct((rows, heads * HEAD_DIM), jnp.bfloat16),
        compiler_params=pltpu.CompilerParams(vmem_limit_bytes=40 * 1024 * 1024),
        cost_estimate=pl.CostEstimate(
            flops=4 * heads * rows * limit * HEAD_DIM,
            bytes_accessed=4 * limit * HEAD_DIM,
            transcendentals=heads * rows * limit,
        ),
        name="attention",
    )(info, queries_t, new_keys, new_values, keys, values)


def tail_kernel(
    groups,
    context,
    base,
    table,
    gain,
    w_out,
    gate,
    up,
    down,
    out_ref,
    ctx_in,
    rows_g,
    rows_p,
    tab_g,
    tab_p,
    keep,
    out_y,
    in_y,
    in_z,
    residual,
    pieces,
    ctx_send,
    ctx_recv,
    row_send,
    row_recv,
    tab_send,
    tab_recv,
    y_send,
    y_recv,
    z_send,
    z_recv,
    end_send,
    end_recv,
):
    tensor_count = lax.axis_size("tensor")
    tensor = lax.axis_index("tensor")
    expert = lax.axis_index("expert")
    group = expert // 2
    side = expert % 2
    partner = (group * 2 + (1 - side), tensor)
    quarter = base.shape[0]
    width = out_ref.shape[1]

    def peer(step):
        return (expert, (tensor + step) % tensor_count)

    def ahead(step):
        return (((group + step) % groups) * 2 + side, tensor)

    def behind(step):
        return (((group + groups - step) % groups) * 2 + side, tensor)

    def remote(source, target, send, recv, device):
        return pltpu.make_async_remote_copy(
            src_ref=source,
            dst_ref=target,
            send_sem=send,
            recv_sem=recv,
            device_id=device,
            device_id_type=pl.DeviceIdType.MESH,
        )

    def context_copy(step):
        place = ((tensor + step) % tensor_count) * quarter
        return remote(
            context.at[pl.ds(pl.multiple_of(place, quarter), quarter)],
            ctx_in.at[step],
            ctx_send.at[step],
            ctx_recv.at[step],
            peer(step),
        )

    def group_copies(step):
        return (
            remote(rows_g.at[0], rows_g.at[step], row_send.at[0, step], row_recv.at[0, step], ahead(step)),
            remote(tab_g.at[0], tab_g.at[step], tab_send.at[0, step], tab_recv.at[0, step], ahead(step)),
        )

    def partner_copies(step):
        return (
            remote(rows_g.at[step], rows_p.at[step], row_send.at[1, step], row_recv.at[1, step], partner),
            remote(tab_g.at[step], tab_p.at[step], tab_send.at[1, step], tab_recv.at[1, step], partner),
        )

    def y_copy(step):
        return remote(out_y.at[step], in_y.at[step], y_send.at[step], y_recv.at[step], partner)

    def z_copy(step):
        return remote(in_y.at[step], in_z.at[step], z_send.at[step], z_recv.at[step], behind(step))

    def end_copy(step):
        place = (tensor + step) % tensor_count
        return remote(
            pieces.at[place],
            out_ref.at[pl.ds(pl.multiple_of(tensor * quarter, quarter), quarter)],
            end_send.at[step],
            end_recv.at[step],
            peer(step),
        )

    barrier = pltpu.get_barrier_semaphore()

    def greet(device):
        pl.semaphore_signal(
            barrier, inc=1, device_id=device, device_id_type=pl.DeviceIdType.MESH
        )

    greet(partner)
    for step in range(1, groups):
        greet(ahead(step))
    for step in range(1, tensor_count):
        greet(peer(step))
    pl.semaphore_wait(barrier, groups + tensor_count - 1)

    for step in range(1, tensor_count):
        context_copy(step).start()
    mine = context[pl.ds(pl.multiple_of(tensor * quarter, quarter), quarter), :]
    total = base[...].astype(jnp.float32) + jnp.dot(
        mine, w_out[tensor], preferred_element_type=jnp.float32
    )
    for step in range(1, tensor_count):
        context_copy(step).wait_recv()
        source = (tensor + tensor_count - step) % tensor_count
        total = total + jnp.dot(ctx_in[step], w_out[source], preferred_element_type=jnp.float32)
    residual[...] = total.astype(jnp.bfloat16)
    values = residual[...].astype(jnp.float32)
    mean_square = jnp.mean(values * values, axis=-1, keepdims=True)
    rows_g[0] = (values * lax.rsqrt(mean_square + epsilon) * gain[...]).astype(jnp.bfloat16)
    tab_g[0] = table[...]

    for step in range(1, groups):
        for copy in group_copies(step):
            copy.start()
    for copy in partner_copies(0):
        copy.start()

    def column(tab):
        place = lax.broadcasted_iota(jnp.int32, tab.shape, 0)
        row = jnp.sum(jnp.where(place == expert, tab, 0.0), axis=0, keepdims=True)
        return jnp.broadcast_to(row, (8, quarter)).T[:, :1]

    def merge(step):
        y_copy(step).wait_recv()
        joined = keep[step % 2] + in_y[step].astype(jnp.float32)
        in_y[step] = joined.astype(jnp.bfloat16)

        @pl.when(step > 0)
        def _():
            z_copy(step).start()

    def visit(step, carry):
        @pl.when(step + 1 < groups)
        def _():
            for copy in group_copies(step + 1):
                copy.wait_recv()
            for copy in partner_copies(step + 1):
                copy.start()

        for copy in partner_copies(step):
            copy.wait_recv()
        rows = jnp.concatenate([rows_g[step], rows_p[step]], axis=0)
        result = None
        for part in range(tensor_count):
            gated = jnp.dot(rows, gate[part], preferred_element_type=jnp.float32)
            upward = jnp.dot(rows, up[part], preferred_element_type=jnp.float32)
            active = (jnp.maximum(gated, 0.0) * upward).astype(jnp.bfloat16)
            term = jnp.dot(active, down[part], preferred_element_type=jnp.float32)
            result = term if result is None else result + term
        out_y[step] = (result[quarter:] * column(tab_p[step])).astype(jnp.bfloat16)
        y_copy(step).start()
        keep[step % 2] = result[:quarter] * column(tab_g[step])

        @pl.when(step > 0)
        def _():
            merge(step - 1)

        return carry

    lax.fori_loop(0, groups, visit, 0)
    merge(groups - 1)

    final = residual[...].astype(jnp.float32) + in_y[0].astype(jnp.float32)
    for step in range(1, groups):
        z_copy(step).wait_recv()
        final = final + in_z[step].astype(jnp.float32)
    final = final.astype(jnp.bfloat16)
    for part in range(tensor_count):
        pieces[part] = final[:, part * width : (part + 1) * width]
    for step in range(1, tensor_count):
        end_copy(step).start()
    out_ref[pl.ds(pl.multiple_of(tensor * quarter, quarter), quarter), :] = pieces[tensor]

    for step in range(1, tensor_count):
        end_copy(step).wait_recv()
        end_copy(step).wait_send()
        context_copy(step).wait_send()
    for step in range(groups):
        for copy in partner_copies(step):
            copy.wait_send()
        y_copy(step).wait_send()
        if step > 0:
            for copy in group_copies(step):
                copy.wait_send()
            z_copy(step).wait_send()


def tail(context, base, table, gain, w_out, gate, up, down):
    groups = lax.axis_size("expert") // 2
    tensor_count = lax.axis_size("tensor")
    quarter, model = base.shape
    width = model // tensor_count
    dma = pltpu.SemaphoreType.DMA
    block = (groups, quarter, model)
    operands = (context, base, table, gain, w_out, gate, up, down)
    return pl.pallas_call(
        functools.partial(tail_kernel, groups),
        out_shape=jax.ShapeDtypeStruct((quarter * tensor_count, width), jnp.bfloat16),
        in_specs=[pl.BlockSpec(memory_space=pltpu.VMEM)] * len(operands),
        out_specs=pl.BlockSpec(memory_space=pltpu.VMEM),
        scratch_shapes=[
            pltpu.VMEM((tensor_count, quarter, context.shape[1]), jnp.bfloat16),
            pltpu.VMEM(block, jnp.bfloat16),
            pltpu.VMEM(block, jnp.bfloat16),
            pltpu.VMEM((groups,) + table.shape, jnp.float32),
            pltpu.VMEM((groups,) + table.shape, jnp.float32),
            pltpu.VMEM((2, quarter, model), jnp.float32),
            pltpu.VMEM(block, jnp.bfloat16),
            pltpu.VMEM(block, jnp.bfloat16),
            pltpu.VMEM(block, jnp.bfloat16),
            pltpu.VMEM((quarter, model), jnp.bfloat16),
            pltpu.VMEM((tensor_count, quarter, width), jnp.bfloat16),
            dma((tensor_count,)),
            dma((tensor_count,)),
            dma((2, groups)),
            dma((2, groups)),
            dma((2, groups)),
            dma((2, groups)),
            dma((groups,)),
            dma((groups,)),
            dma((groups,)),
            dma((groups,)),
            dma((tensor_count,)),
            dma((tensor_count,)),
        ],
        compiler_params=pltpu.CompilerParams(
            collective_id=0, has_side_effects=True, vmem_limit_bytes=56 * 1024 * 1024
        ),
        name="tail",
    )(*operands)


def local(
    hidden_in,
    cache_lengths,
    new_lengths,
    key_cache,
    cached_value_rows,
    attn_gain,
    w_query,
    key_matrix,
    value_matrix,
    w_out,
    moe_gain,
    route_ids,
    route_weights,
    w_gate,
    w_up,
    w_down,
):
    tensor_count = lax.axis_size("tensor")
    tensor_index = lax.axis_index("tensor")
    new_count = hidden_in.shape[0]
    quarter = new_count // tensor_count
    local_heads = w_query.shape[1] // HEAD_DIM
    query_group_count = QUERY_HEADS // KEY_VALUE_HEADS
    shared = tensor_index * local_heads // query_group_count
    expert_total = w_gate.shape[0] * lax.axis_size("expert")

    full_rows = lax.all_gather(hidden_in, "tensor", axis=1, tiled=True)
    whole_out = lax.all_gather(w_out, "tensor", axis=0, tiled=False)
    whole_gate = lax.all_gather(w_gate[0], "tensor", axis=0, tiled=False)
    whole_up = lax.all_gather(w_up[0], "tensor", axis=0, tiled=False)
    whole_down = lax.all_gather(w_down[0], "tensor", axis=0, tiled=False)

    my_ids = lax.dynamic_slice_in_dim(route_ids, tensor_index * quarter, quarter, 0)
    my_weights = lax.dynamic_slice_in_dim(route_weights, tensor_index * quarter, quarter, 0)
    named = my_ids.T[:, None, :] == jnp.arange(expert_total, dtype=jnp.int32)[None, :, None]
    table = jnp.sum(jnp.where(named, my_weights.T[:, None, :], 0.0), axis=0)

    attn_in = norm_rows(full_rows, attn_gain)
    queries_t = lax.dot_general(
        w_query, attn_in, (((0,), (1,)), ((), ())), preferred_element_type=jnp.float32
    ).astype(jnp.bfloat16)
    key_weight = lax.dynamic_slice_in_dim(key_matrix, shared * HEAD_DIM, HEAD_DIM, 1)
    value_weight = lax.dynamic_slice_in_dim(value_matrix, shared * HEAD_DIM, HEAD_DIM, 1)
    both = jnp.dot(
        attn_in,
        jnp.concatenate([key_weight, value_weight], axis=1),
        preferred_element_type=jnp.float32,
    ).astype(jnp.bfloat16)
    context = attention(
        queries_t,
        both[:, :HEAD_DIM],
        both[:, HEAD_DIM:],
        key_cache,
        cached_value_rows,
        cache_lengths[0],
        new_lengths[0],
        shared,
    )
    my_rows = lax.dynamic_slice_in_dim(full_rows, tensor_index * quarter, quarter, 0)
    return tail(
        context,
        my_rows,
        table,
        moe_gain[None, :],
        whole_out,
        whole_gate,
        whole_up,
        whole_down,
    )


def solution(mesh):
    placed = (
        P("expert", "tensor"),
        P("expert"),
        P("expert"),
        P("expert", None, None),
        P("expert", None, None),
        P(),
        P(None, "tensor"),
        P(),
        P(),
        P("tensor", None),
        P(),
        P("expert", None),
        P("expert", None),
        P("expert", None, "tensor"),
        P("expert", None, "tensor"),
        P("expert", "tensor", None),
    )
    return jax.shard_map(
        local, mesh=mesh, in_specs=placed, out_specs=P("expert", "tensor"), check_vma=False
    )
```

```python
import functools
import math

import jax
import jax.numpy as jnp
from jax import lax
from jax.experimental import pallas as pl
from jax.experimental.pallas import tpu as pltpu
from jax.sharding import PartitionSpec as P

QUERY_HEADS = 12
KEY_VALUE_HEADS = 2
HEAD_DIM = 128
TOP = 4
BLOCK = 1024

epsilon = 1e-06


def norm_rows(activity, gain_vector):
    values = activity.astype(jnp.float32)
    mean_square = jnp.mean(values * values, axis=-1, keepdims=True)
    return (values * lax.rsqrt(mean_square + epsilon) * gain_vector).astype(jnp.bfloat16)


def attention_kernel(
    heads, scale, info, q_ref, nk_ref, nv_ref, k_ref, v_ref, out_ref, top, total, acc
):
    step = pl.program_id(0)
    length = info[0]
    fresh = info[1]
    block = k_ref.shape[1]
    rows = q_ref.shape[1]

    def visit(head, keys, values, mask, first):
        scores = jnp.dot(
            keys,
            q_ref[head * HEAD_DIM : (head + 1) * HEAD_DIM, :],
            preferred_element_type=jnp.float32,
        )
        if mask is not None:
            scores = jnp.where(mask, scores, -jnp.inf)
        largest = jnp.max(scores, axis=0, keepdims=True)
        if not first:
            before = top[head : head + 1, :]
            largest = jnp.maximum(largest, before)
        weights = jnp.exp2((scores - largest) * scale)
        added = jnp.sum(weights, axis=0, keepdims=True)
        product = lax.dot_general(
            values,
            weights.astype(jnp.bfloat16),
            (((0,), (0,)), ((), ())),
            preferred_element_type=jnp.float32,
        )
        if not first:
            alpha = jnp.exp2((before - largest) * scale)
            added = added + total[head : head + 1, :] * alpha
            product = product + acc[head] * alpha
        top[head : head + 1, :] = largest
        total[head : head + 1, :] = added
        acc[head] = product

    @pl.when(step == 0)
    def _():
        count = nk_ref.shape[0]
        key_place = lax.broadcasted_iota(jnp.int32, (count, rows), 0)
        query_place = lax.broadcasted_iota(jnp.int32, (count, rows), 1)
        mask = (key_place <= query_place) & (key_place < fresh)
        for head in range(heads):
            visit(head, nk_ref[...], nv_ref[...], mask, True)

    start = (step - 1) * block

    @pl.when((step > 0) & (start + block <= length))
    def _():
        for head in range(heads):
            visit(head, k_ref[0], v_ref[0], None, False)

    @pl.when((step > 0) & (start < length) & (start + block > length))
    def _():
        place = lax.broadcasted_iota(jnp.int32, (block, rows), 0) + start
        for head in range(heads):
            visit(head, k_ref[0], v_ref[0], place < length, False)

    @pl.when(step == pl.num_programs(0) - 1)
    def _():
        for head in range(heads):
            result = acc[head] / total[head : head + 1, :]
            out_ref[:, head * HEAD_DIM : (head + 1) * HEAD_DIM] = result.T.astype(jnp.bfloat16)


def attention(queries_t, new_keys, new_values, keys, values, length, fresh, shared):
    heads = queries_t.shape[0] // HEAD_DIM
    rows = queries_t.shape[1]
    limit = keys.shape[1]
    block = min(BLOCK, limit)
    scale = math.log2(math.e) / math.sqrt(HEAD_DIM)
    info = jnp.stack([length, fresh, shared]).astype(jnp.int32)

    def place(step, info):
        last = jnp.maximum((info[0] + block - 1) // block - 1, 0)
        return (0, jnp.minimum(jnp.maximum(step - 1, 0), last), info[2])

    return pl.pallas_call(
        functools.partial(attention_kernel, heads, scale),
        grid_spec=pltpu.PrefetchScalarGridSpec(
            num_scalar_prefetch=1,
            grid=(1 + limit // block,),
            in_specs=[
                pl.BlockSpec(queries_t.shape, lambda step, info: (0, 0)),
                pl.BlockSpec(new_keys.shape, lambda step, info: (0, 0)),
                pl.BlockSpec(new_values.shape, lambda step, info: (0, 0)),
                pl.BlockSpec((1, block, HEAD_DIM), place),
                pl.BlockSpec((1, block, HEAD_DIM), place),
            ],
            out_specs=pl.BlockSpec((rows, heads * HEAD_DIM), lambda step, info: (0, 0)),
            scratch_shapes=[
                pltpu.VMEM((8, rows), jnp.float32),
                pltpu.VMEM((8, rows), jnp.float32),
                pltpu.VMEM((heads, HEAD_DIM, rows), jnp.float32),
            ],
        ),
        out_shape=jax.ShapeDtypeStruct((rows, heads * HEAD_DIM), jnp.bfloat16),
        compiler_params=pltpu.CompilerParams(vmem_limit_bytes=40 * 1024 * 1024),
        cost_estimate=pl.CostEstimate(
            flops=4 * heads * rows * limit * HEAD_DIM,
            bytes_accessed=4 * limit * HEAD_DIM,
            transcendentals=heads * rows * limit,
        ),
        name="attention",
    )(info, queries_t, new_keys, new_values, keys, values)


def tail_kernel(
    groups,
    context,
    base,
    table,
    gain,
    w_out,
    gate_part,
    up_part,
    down_part,
    out_ref,
    gate,
    up,
    down,
    ctx_in,
    rows_g,
    rows_p,
    tab_g,
    tab_p,
    keep,
    out_y,
    in_y,
    in_z,
    residual,
    pieces,
    ctx_send,
    ctx_recv,
    row_send,
    row_recv,
    tab_send,
    tab_recv,
    y_send,
    y_recv,
    z_send,
    z_recv,
    end_send,
    end_recv,
    weight_send,
    weight_recv,
):
    tensor_count = lax.axis_size("tensor")
    tensor = lax.axis_index("tensor")
    expert = lax.axis_index("expert")
    group = expert // 2
    side = expert % 2
    partner = (group * 2 + (1 - side), tensor)
    quarter = base.shape[0]
    width = out_ref.shape[1]

    def peer(step):
        return (expert, (tensor + step) % tensor_count)

    def ahead(step):
        return (((group + step) % groups) * 2 + side, tensor)

    def behind(step):
        return (((group + groups - step) % groups) * 2 + side, tensor)

    def remote(source, target, send, recv, device):
        return pltpu.make_async_remote_copy(
            src_ref=source,
            dst_ref=target,
            send_sem=send,
            recv_sem=recv,
            device_id=device,
            device_id_type=pl.DeviceIdType.MESH,
        )

    def context_copy(step):
        place = ((tensor + step) % tensor_count) * quarter
        return remote(
            context.at[pl.ds(pl.multiple_of(place, quarter), quarter)],
            ctx_in.at[step],
            ctx_send.at[step],
            ctx_recv.at[step],
            peer(step),
        )

    def group_copies(step):
        return (
            remote(rows_g.at[0], rows_g.at[step], row_send.at[0, step], row_recv.at[0, step], ahead(step)),
            remote(tab_g.at[0], tab_g.at[step], tab_send.at[0, step], tab_recv.at[0, step], ahead(step)),
        )

    def partner_copies(step):
        return (
            remote(rows_g.at[step], rows_p.at[step], row_send.at[1, step], row_recv.at[1, step], partner),
            remote(tab_g.at[step], tab_p.at[step], tab_send.at[1, step], tab_recv.at[1, step], partner),
        )

    sibling = (tensor // 2) * 2 + (1 - tensor % 2)
    across = (tensor + 2) % tensor_count
    shards = ((gate_part, gate), (up_part, up), (down_part, down))

    def weight_copy(number, leg):
        shard, whole = shards[number]
        slot = across if leg == 2 else tensor
        source = whole.at[slot] if leg == 2 else shard
        return remote(
            source,
            whole.at[slot],
            weight_send.at[number, leg],
            weight_recv.at[number, leg],
            (expert, across if leg == 1 else sibling),
        )

    def y_copy(step):
        return remote(out_y.at[step], in_y.at[step], y_send.at[step], y_recv.at[step], partner)

    def z_copy(step):
        return remote(in_y.at[step], in_z.at[step], z_send.at[step], z_recv.at[step], behind(step))

    def end_copy(step):
        place = (tensor + step) % tensor_count
        return remote(
            pieces.at[place],
            out_ref.at[pl.ds(pl.multiple_of(tensor * quarter, quarter), quarter)],
            end_send.at[step],
            end_recv.at[step],
            peer(step),
        )

    barrier = pltpu.get_barrier_semaphore()

    def greet(device):
        pl.semaphore_signal(
            barrier, inc=1, device_id=device, device_id_type=pl.DeviceIdType.MESH
        )

    greet(partner)
    for step in range(1, groups):
        greet(ahead(step))
    for step in range(1, tensor_count):
        greet(peer(step))
    pl.semaphore_wait(barrier, groups + tensor_count - 1)

    for step in range(1, tensor_count):
        context_copy(step).start()
    for number in range(3):
        weight_copy(number, 1).start()
    for number in range(3):
        weight_copy(number, 0).start()
    mine = context[pl.ds(pl.multiple_of(tensor * quarter, quarter), quarter), :]
    total = base[...].astype(jnp.float32) + jnp.dot(
        mine, w_out[tensor], preferred_element_type=jnp.float32
    )
    for step in range(1, tensor_count):
        context_copy(step).wait_recv()
        source = (tensor + tensor_count - step) % tensor_count
        total = total + jnp.dot(ctx_in[step], w_out[source], preferred_element_type=jnp.float32)
    residual[...] = total.astype(jnp.bfloat16)
    values = residual[...].astype(jnp.float32)
    mean_square = jnp.mean(values * values, axis=-1, keepdims=True)
    rows_g[0] = (values * lax.rsqrt(mean_square + epsilon) * gain[...]).astype(jnp.bfloat16)
    tab_g[0] = table[...]

    for step in range(1, groups):
        for copy in group_copies(step):
            copy.start()
    for copy in partner_copies(0):
        copy.start()

    def column(tab):
        place = lax.broadcasted_iota(jnp.int32, tab.shape, 0)
        row = jnp.sum(jnp.where(place == expert, tab, 0.0), axis=0, keepdims=True)
        return jnp.broadcast_to(row, (8, quarter)).T[:, :1]

    def merge(step):
        y_copy(step).wait_recv()
        joined = keep[step % 2] + in_y[step].astype(jnp.float32)
        in_y[step] = joined.astype(jnp.bfloat16)

        @pl.when(step > 0)
        def _():
            z_copy(step).start()

    for number in range(3):
        shard, whole = shards[number]
        whole[tensor] = shard[...]

    def forward(step):
        for copy in group_copies(step):
            copy.wait_recv()
        for copy in partner_copies(step):
            copy.start()

    for step in range(1, groups):
        forward(step)
        if step <= 3:
            weight_copy(step - 1, 1).wait_recv()
            weight_copy(step - 1, 2).start()
    for number in range(min(groups - 1, 3), 3):
        weight_copy(number, 1).wait_recv()
        weight_copy(number, 2).start()
    for number in range(3):
        weight_copy(number, 0).wait_recv()
        weight_copy(number, 2).wait_recv()

    def visit(step, carry):
        for copy in partner_copies(step):
            copy.wait_recv()
        rows = jnp.concatenate([rows_g[step], rows_p[step]], axis=0)
        result = None
        for part in range(tensor_count):
            gated = jnp.dot(rows, gate[part], preferred_element_type=jnp.float32)
            upward = jnp.dot(rows, up[part], preferred_element_type=jnp.float32)
            active = (jnp.maximum(gated, 0.0) * upward).astype(jnp.bfloat16)
            term = jnp.dot(active, down[part], preferred_element_type=jnp.float32)
            result = term if result is None else result + term
        out_y[step] = (result[quarter:] * column(tab_p[step])).astype(jnp.bfloat16)
        y_copy(step).start()
        keep[step % 2] = result[:quarter] * column(tab_g[step])

        @pl.when(step > 0)
        def _():
            merge(step - 1)

        return carry

    lax.fori_loop(0, groups, visit, 0)
    merge(groups - 1)

    final = residual[...].astype(jnp.float32) + in_y[0].astype(jnp.float32)
    for step in range(1, groups):
        z_copy(step).wait_recv()
        final = final + in_z[step].astype(jnp.float32)
    final = final.astype(jnp.bfloat16)
    for part in range(tensor_count):
        pieces[part] = final[:, part * width : (part + 1) * width]
    for step in range(1, tensor_count):
        end_copy(step).start()
    out_ref[pl.ds(pl.multiple_of(tensor * quarter, quarter), quarter), :] = pieces[tensor]

    for step in range(1, tensor_count):
        end_copy(step).wait_recv()
        end_copy(step).wait_send()
        context_copy(step).wait_send()
    for number in range(3):
        for leg in range(3):
            weight_copy(number, leg).wait_send()
    for step in range(groups):
        for copy in partner_copies(step):
            copy.wait_send()
        y_copy(step).wait_send()
        if step > 0:
            for copy in group_copies(step):
                copy.wait_send()
            z_copy(step).wait_send()


def tail(context, base, table, gain, w_out, gate, up, down):
    groups = lax.axis_size("expert") // 2
    tensor_count = lax.axis_size("tensor")
    quarter, model = base.shape
    width = model // tensor_count
    dma = pltpu.SemaphoreType.DMA
    block = (groups, quarter, model)
    operands = (context, base, table, gain, w_out, gate, up, down)
    return pl.pallas_call(
        functools.partial(tail_kernel, groups),
        out_shape=jax.ShapeDtypeStruct((quarter * tensor_count, width), jnp.bfloat16),
        in_specs=[pl.BlockSpec(memory_space=pltpu.VMEM)] * len(operands),
        out_specs=pl.BlockSpec(memory_space=pltpu.VMEM),
        scratch_shapes=[
            pltpu.VMEM((tensor_count,) + gate.shape, jnp.bfloat16),
            pltpu.VMEM((tensor_count,) + up.shape, jnp.bfloat16),
            pltpu.VMEM((tensor_count,) + down.shape, jnp.bfloat16),
            pltpu.VMEM((tensor_count, quarter, context.shape[1]), jnp.bfloat16),
            pltpu.VMEM(block, jnp.bfloat16),
            pltpu.VMEM(block, jnp.bfloat16),
            pltpu.VMEM((groups,) + table.shape, jnp.float32),
            pltpu.VMEM((groups,) + table.shape, jnp.float32),
            pltpu.VMEM((2, quarter, model), jnp.float32),
            pltpu.VMEM(block, jnp.bfloat16),
            pltpu.VMEM(block, jnp.bfloat16),
            pltpu.VMEM(block, jnp.bfloat16),
            pltpu.VMEM((quarter, model), jnp.bfloat16),
            pltpu.VMEM((tensor_count, quarter, width), jnp.bfloat16),
            dma((tensor_count,)),
            dma((tensor_count,)),
            dma((2, groups)),
            dma((2, groups)),
            dma((2, groups)),
            dma((2, groups)),
            dma((groups,)),
            dma((groups,)),
            dma((groups,)),
            dma((groups,)),
            dma((tensor_count,)),
            dma((tensor_count,)),
            dma((3, 3)),
            dma((3, 3)),
        ],
        compiler_params=pltpu.CompilerParams(
            collective_id=0, has_side_effects=True, vmem_limit_bytes=56 * 1024 * 1024
        ),
        name="tail",
    )(*operands)


def local(
    hidden_in,
    cache_lengths,
    new_lengths,
    key_cache,
    cached_value_rows,
    attn_gain,
    w_query,
    key_matrix,
    value_matrix,
    w_out,
    moe_gain,
    route_ids,
    route_weights,
    w_gate,
    w_up,
    w_down,
):
    tensor_count = lax.axis_size("tensor")
    tensor_index = lax.axis_index("tensor")
    new_count = hidden_in.shape[0]
    quarter = new_count // tensor_count
    local_heads = w_query.shape[1] // HEAD_DIM
    query_group_count = QUERY_HEADS // KEY_VALUE_HEADS
    shared = tensor_index * local_heads // query_group_count
    expert_total = w_gate.shape[0] * lax.axis_size("expert")

    full_rows = lax.all_gather(hidden_in, "tensor", axis=1, tiled=True)
    whole_out = lax.all_gather(w_out, "tensor", axis=0, tiled=False)

    my_ids = lax.dynamic_slice_in_dim(route_ids, tensor_index * quarter, quarter, 0)
    my_weights = lax.dynamic_slice_in_dim(route_weights, tensor_index * quarter, quarter, 0)
    named = my_ids.T[:, None, :] == jnp.arange(expert_total, dtype=jnp.int32)[None, :, None]
    table = jnp.sum(jnp.where(named, my_weights.T[:, None, :], 0.0), axis=0)

    attn_in = norm_rows(full_rows, attn_gain)
    queries_t = lax.dot_general(
        w_query, attn_in, (((0,), (1,)), ((), ())), preferred_element_type=jnp.float32
    ).astype(jnp.bfloat16)
    key_weight = lax.dynamic_slice_in_dim(key_matrix, shared * HEAD_DIM, HEAD_DIM, 1)
    value_weight = lax.dynamic_slice_in_dim(value_matrix, shared * HEAD_DIM, HEAD_DIM, 1)
    both = jnp.dot(
        attn_in,
        jnp.concatenate([key_weight, value_weight], axis=1),
        preferred_element_type=jnp.float32,
    ).astype(jnp.bfloat16)
    context = attention(
        queries_t,
        both[:, :HEAD_DIM],
        both[:, HEAD_DIM:],
        key_cache,
        cached_value_rows,
        cache_lengths[0],
        new_lengths[0],
        shared,
    )
    my_rows = lax.dynamic_slice_in_dim(full_rows, tensor_index * quarter, quarter, 0)
    return tail(
        context,
        my_rows,
        table,
        moe_gain[None, :],
        whole_out,
        w_gate[0],
        w_up[0],
        w_down[0],
    )


def solution(mesh):
    placed = (
        P("expert", "tensor"),
        P("expert"),
        P("expert"),
        P("expert", None, None),
        P("expert", None, None),
        P(),
        P(None, "tensor"),
        P(),
        P(),
        P("tensor", None),
        P(),
        P("expert", None),
        P("expert", None),
        P("expert", None, "tensor"),
        P("expert", None, "tensor"),
        P("expert", "tensor", None),
    )
    return jax.shard_map(
        local, mesh=mesh, in_specs=placed, out_specs=P("expert", "tensor"), check_vma=False
    )
```

```python
import functools
import math

import jax
import jax.numpy as jnp
from jax import lax
from jax.experimental import pallas as pl
from jax.experimental.pallas import tpu as pltpu
from jax.sharding import PartitionSpec as P

QUERY_HEADS = 12
KEY_VALUE_HEADS = 2
HEAD_DIM = 128
TOP = 4
BLOCK = 1024

epsilon = 1e-06


def norm_rows(activity, gain_vector):
    values = activity.astype(jnp.float32)
    mean_square = jnp.mean(values * values, axis=-1, keepdims=True)
    return (values * lax.rsqrt(mean_square + epsilon) * gain_vector).astype(jnp.bfloat16)


def attention_kernel(
    heads, scale, info, q_ref, nk_ref, nv_ref, k_ref, v_ref, out_ref, top, total, acc
):
    step = pl.program_id(0)
    length = info[0]
    fresh = info[1]
    block = k_ref.shape[1]
    rows = q_ref.shape[1]

    def visit(head, keys, values, mask, first):
        scores = jnp.dot(
            keys,
            q_ref[head * HEAD_DIM : (head + 1) * HEAD_DIM, :],
            preferred_element_type=jnp.float32,
        )
        if mask is not None:
            scores = jnp.where(mask, scores, -jnp.inf)
        largest = jnp.max(scores, axis=0, keepdims=True)
        if not first:
            before = top[head : head + 1, :]
            largest = jnp.maximum(largest, before)
        weights = jnp.exp2((scores - largest) * scale)
        added = jnp.sum(weights, axis=0, keepdims=True)
        product = lax.dot_general(
            values,
            weights.astype(jnp.bfloat16),
            (((0,), (0,)), ((), ())),
            preferred_element_type=jnp.float32,
        )
        if not first:
            alpha = jnp.exp2((before - largest) * scale)
            added = added + total[head : head + 1, :] * alpha
            product = product + acc[head] * alpha
        top[head : head + 1, :] = largest
        total[head : head + 1, :] = added
        acc[head] = product

    @pl.when(step == 0)
    def _():
        count = nk_ref.shape[0]
        key_place = lax.broadcasted_iota(jnp.int32, (count, rows), 0)
        query_place = lax.broadcasted_iota(jnp.int32, (count, rows), 1)
        mask = (key_place <= query_place) & (key_place < fresh)
        for head in range(heads):
            visit(head, nk_ref[...], nv_ref[...], mask, True)

    start = (step - 1) * block

    @pl.when((step > 0) & (start + block <= length))
    def _():
        for head in range(heads):
            visit(head, k_ref[0], v_ref[0], None, False)

    @pl.when((step > 0) & (start < length) & (start + block > length))
    def _():
        place = lax.broadcasted_iota(jnp.int32, (block, rows), 0) + start
        for head in range(heads):
            visit(head, k_ref[0], v_ref[0], place < length, False)

    @pl.when(step == pl.num_programs(0) - 1)
    def _():
        for head in range(heads):
            result = acc[head] / total[head : head + 1, :]
            out_ref[:, head * HEAD_DIM : (head + 1) * HEAD_DIM] = result.T.astype(jnp.bfloat16)


def attention(queries_t, new_keys, new_values, keys, values, length, fresh, shared):
    heads = queries_t.shape[0] // HEAD_DIM
    rows = queries_t.shape[1]
    limit = keys.shape[1]
    block = min(BLOCK, limit)
    scale = math.log2(math.e) / math.sqrt(HEAD_DIM)
    info = jnp.stack([length, fresh, shared]).astype(jnp.int32)

    def place(step, info):
        last = jnp.maximum((info[0] + block - 1) // block - 1, 0)
        return (0, jnp.minimum(jnp.maximum(step - 1, 0), last), info[2])

    return pl.pallas_call(
        functools.partial(attention_kernel, heads, scale),
        grid_spec=pltpu.PrefetchScalarGridSpec(
            num_scalar_prefetch=1,
            grid=(1 + limit // block,),
            in_specs=[
                pl.BlockSpec(queries_t.shape, lambda step, info: (0, 0)),
                pl.BlockSpec(new_keys.shape, lambda step, info: (0, 0)),
                pl.BlockSpec(new_values.shape, lambda step, info: (0, 0)),
                pl.BlockSpec((1, block, HEAD_DIM), place),
                pl.BlockSpec((1, block, HEAD_DIM), place),
            ],
            out_specs=pl.BlockSpec((rows, heads * HEAD_DIM), lambda step, info: (0, 0)),
            scratch_shapes=[
                pltpu.VMEM((8, rows), jnp.float32),
                pltpu.VMEM((8, rows), jnp.float32),
                pltpu.VMEM((heads, HEAD_DIM, rows), jnp.float32),
            ],
        ),
        out_shape=jax.ShapeDtypeStruct((rows, heads * HEAD_DIM), jnp.bfloat16),
        compiler_params=pltpu.CompilerParams(vmem_limit_bytes=40 * 1024 * 1024),
        cost_estimate=pl.CostEstimate(
            flops=4 * heads * rows * limit * HEAD_DIM,
            bytes_accessed=4 * limit * HEAD_DIM,
            transcendentals=heads * rows * limit,
        ),
        name="attention",
    )(info, queries_t, new_keys, new_values, keys, values)


def tail_kernel(
    groups,
    context,
    base,
    table,
    gain,
    w_out,
    gate_part,
    up_part,
    down_part,
    out_ref,
    gate,
    up,
    down,
    ctx_in,
    rows_g,
    rows_p,
    tab_g,
    tab_p,
    keep,
    out_y,
    in_y,
    in_z,
    residual,
    pieces,
    ctx_send,
    ctx_recv,
    row_send,
    row_recv,
    tab_send,
    tab_recv,
    y_send,
    y_recv,
    z_send,
    z_recv,
    end_send,
    end_recv,
    weight_send,
    weight_recv,
):
    tensor_count = lax.axis_size("tensor")
    tensor = lax.axis_index("tensor")
    expert = lax.axis_index("expert")
    group = expert // 2
    side = expert % 2
    partner = (group * 2 + (1 - side), tensor)
    quarter = base.shape[0]
    width = out_ref.shape[1]

    def peer(step):
        return (expert, (tensor + step) % tensor_count)

    def ahead(step):
        return (((group + step) % groups) * 2 + side, tensor)

    def behind(step):
        return (((group + groups - step) % groups) * 2 + side, tensor)

    def remote(source, target, send, recv, device):
        return pltpu.make_async_remote_copy(
            src_ref=source,
            dst_ref=target,
            send_sem=send,
            recv_sem=recv,
            device_id=device,
            device_id_type=pl.DeviceIdType.MESH,
        )

    def context_copy(step):
        place = ((tensor + step) % tensor_count) * quarter
        return remote(
            context.at[pl.ds(pl.multiple_of(place, quarter), quarter)],
            ctx_in.at[step],
            ctx_send.at[step],
            ctx_recv.at[step],
            peer(step),
        )

    def group_copies(step):
        return (
            remote(rows_g.at[0], rows_g.at[step], row_send.at[0, step], row_recv.at[0, step], ahead(step)),
            remote(tab_g.at[0], tab_g.at[step], tab_send.at[0, step], tab_recv.at[0, step], ahead(step)),
        )

    def partner_copies(step):
        return (
            remote(rows_g.at[step], rows_p.at[step], row_send.at[1, step], row_recv.at[1, step], partner),
            remote(tab_g.at[step], tab_p.at[step], tab_send.at[1, step], tab_recv.at[1, step], partner),
        )

    sibling = (tensor // 2) * 2 + (1 - tensor % 2)
    across = (tensor + 2) % tensor_count
    shards = ((gate_part, gate), (up_part, up), (down_part, down))

    def weight_copy(number, leg):
        shard, whole = shards[number]
        slot = across if leg == 2 else tensor
        source = whole.at[slot] if leg == 2 else shard
        return remote(
            source,
            whole.at[slot],
            weight_send.at[number, leg],
            weight_recv.at[number, leg],
            (expert, across if leg == 1 else sibling),
        )

    def y_copy(step):
        return remote(out_y.at[step], in_y.at[step], y_send.at[step], y_recv.at[step], partner)

    def z_copy(step):
        return remote(in_y.at[step], in_z.at[step], z_send.at[step], z_recv.at[step], behind(step))

    def end_copy(step):
        place = (tensor + step) % tensor_count
        return remote(
            pieces.at[place],
            out_ref.at[pl.ds(pl.multiple_of(tensor * quarter, quarter), quarter)],
            end_send.at[step],
            end_recv.at[step],
            peer(step),
        )

    barrier = pltpu.get_barrier_semaphore()

    def greet(device):
        pl.semaphore_signal(
            barrier, inc=1, device_id=device, device_id_type=pl.DeviceIdType.MESH
        )

    greet(partner)
    for step in range(1, groups):
        greet(ahead(step))
    for step in range(1, tensor_count):
        greet(peer(step))
    pl.semaphore_wait(barrier, groups + tensor_count - 1)

    for step in range(1, tensor_count):
        context_copy(step).start()
    for number in range(3):
        weight_copy(number, 1).start()
    for number in range(3):
        weight_copy(number, 0).start()
    mine = context[pl.ds(pl.multiple_of(tensor * quarter, quarter), quarter), :]
    total = base[...].astype(jnp.float32) + jnp.dot(
        mine, w_out[tensor], preferred_element_type=jnp.float32
    )
    for step in range(1, tensor_count):
        context_copy(step).wait_recv()
        source = (tensor + tensor_count - step) % tensor_count
        total = total + jnp.dot(ctx_in[step], w_out[source], preferred_element_type=jnp.float32)
    residual[...] = total.astype(jnp.bfloat16)
    values = residual[...].astype(jnp.float32)
    mean_square = jnp.mean(values * values, axis=-1, keepdims=True)
    rows_g[0] = (values * lax.rsqrt(mean_square + epsilon) * gain[...]).astype(jnp.bfloat16)
    tab_g[0] = table[...]

    for step in range(1, groups):
        for copy in group_copies(step):
            copy.start()
    for copy in partner_copies(0):
        copy.start()

    def column(tab):
        place = lax.broadcasted_iota(jnp.int32, tab.shape, 0)
        row = jnp.sum(jnp.where(place == expert, tab, 0.0), axis=0, keepdims=True)
        return jnp.broadcast_to(row, (8, quarter)).T[:, :1]

    def joined(step, turn):
        y_copy(step).wait_recv()
        return keep[turn % 2] + in_y[step].astype(jnp.float32)

    for number in range(3):
        shard, whole = shards[number]
        whole[tensor] = shard[...]

    def forward(step):
        for copy in group_copies(step):
            copy.wait_recv()
        for copy in partner_copies(step):
            copy.start()

    for step in range(1, groups):
        forward(step)
        if step <= 3:
            weight_copy(step - 1, 1).wait_recv()
            weight_copy(step - 1, 2).start()
    for number in range(min(groups - 1, 3), 3):
        weight_copy(number, 1).wait_recv()
        weight_copy(number, 2).start()
    for number in range(3):
        weight_copy(number, 0).wait_recv()
        weight_copy(number, 2).wait_recv()

    def visit(turn, carry):
        step = (turn + 1) % groups
        for copy in partner_copies(step):
            copy.wait_recv()
        rows = jnp.concatenate([rows_g[step], rows_p[step]], axis=0)
        result = None
        for part in range(tensor_count):
            gated = jnp.dot(rows, gate[part], preferred_element_type=jnp.float32)
            upward = jnp.dot(rows, up[part], preferred_element_type=jnp.float32)
            active = (jnp.maximum(gated, 0.0) * upward).astype(jnp.bfloat16)
            term = jnp.dot(active, down[part], preferred_element_type=jnp.float32)
            result = term if result is None else result + term
        out_y[step] = (result[quarter:] * column(tab_p[step])).astype(jnp.bfloat16)
        y_copy(step).start()
        keep[turn % 2] = result[:quarter] * column(tab_g[step])

        @pl.when(turn > 0)
        def _():
            in_y[turn] = joined(turn, turn - 1).astype(jnp.bfloat16)
            z_copy(turn).start()

        return carry

    lax.fori_loop(0, groups, visit, 0)
    final = residual[...].astype(jnp.float32) + joined(0, groups - 1)
    for step in range(1, groups):
        z_copy(step).wait_recv()
        final = final + in_z[step].astype(jnp.float32)
    final = final.astype(jnp.bfloat16)
    for part in range(tensor_count):
        pieces[part] = final[:, part * width : (part + 1) * width]
    for step in range(1, tensor_count):
        end_copy(step).start()
    out_ref[pl.ds(pl.multiple_of(tensor * quarter, quarter), quarter), :] = pieces[tensor]

    for step in range(1, tensor_count):
        end_copy(step).wait_recv()
        end_copy(step).wait_send()
        context_copy(step).wait_send()
    for number in range(3):
        for leg in range(3):
            weight_copy(number, leg).wait_send()
    for step in range(groups):
        for copy in partner_copies(step):
            copy.wait_send()
        y_copy(step).wait_send()
        if step > 0:
            for copy in group_copies(step):
                copy.wait_send()
            z_copy(step).wait_send()


def tail(context, base, table, gain, w_out, gate, up, down):
    groups = lax.axis_size("expert") // 2
    tensor_count = lax.axis_size("tensor")
    quarter, model = base.shape
    width = model // tensor_count
    dma = pltpu.SemaphoreType.DMA
    block = (groups, quarter, model)
    operands = (context, base, table, gain, w_out, gate, up, down)
    return pl.pallas_call(
        functools.partial(tail_kernel, groups),
        out_shape=jax.ShapeDtypeStruct((quarter * tensor_count, width), jnp.bfloat16),
        in_specs=[pl.BlockSpec(memory_space=pltpu.VMEM)] * len(operands),
        out_specs=pl.BlockSpec(memory_space=pltpu.VMEM),
        scratch_shapes=[
            pltpu.VMEM((tensor_count,) + gate.shape, jnp.bfloat16),
            pltpu.VMEM((tensor_count,) + up.shape, jnp.bfloat16),
            pltpu.VMEM((tensor_count,) + down.shape, jnp.bfloat16),
            pltpu.VMEM((tensor_count, quarter, context.shape[1]), jnp.bfloat16),
            pltpu.VMEM(block, jnp.bfloat16),
            pltpu.VMEM(block, jnp.bfloat16),
            pltpu.VMEM((groups,) + table.shape, jnp.float32),
            pltpu.VMEM((groups,) + table.shape, jnp.float32),
            pltpu.VMEM((2, quarter, model), jnp.float32),
            pltpu.VMEM(block, jnp.bfloat16),
            pltpu.VMEM(block, jnp.bfloat16),
            pltpu.VMEM(block, jnp.bfloat16),
            pltpu.VMEM((quarter, model), jnp.bfloat16),
            pltpu.VMEM((tensor_count, quarter, width), jnp.bfloat16),
            dma((tensor_count,)),
            dma((tensor_count,)),
            dma((2, groups)),
            dma((2, groups)),
            dma((2, groups)),
            dma((2, groups)),
            dma((groups,)),
            dma((groups,)),
            dma((groups,)),
            dma((groups,)),
            dma((tensor_count,)),
            dma((tensor_count,)),
            dma((3, 3)),
            dma((3, 3)),
        ],
        compiler_params=pltpu.CompilerParams(
            collective_id=0, has_side_effects=True, vmem_limit_bytes=56 * 1024 * 1024
        ),
        name="tail",
    )(*operands)


def local(
    hidden_in,
    cache_lengths,
    new_lengths,
    key_cache,
    cached_value_rows,
    attn_gain,
    w_query,
    key_matrix,
    value_matrix,
    w_out,
    moe_gain,
    route_ids,
    route_weights,
    w_gate,
    w_up,
    w_down,
):
    tensor_count = lax.axis_size("tensor")
    tensor_index = lax.axis_index("tensor")
    new_count = hidden_in.shape[0]
    quarter = new_count // tensor_count
    local_heads = w_query.shape[1] // HEAD_DIM
    query_group_count = QUERY_HEADS // KEY_VALUE_HEADS
    shared = tensor_index * local_heads // query_group_count
    expert_total = w_gate.shape[0] * lax.axis_size("expert")

    full_rows = lax.all_gather(hidden_in, "tensor", axis=1, tiled=True)
    whole_out = lax.all_gather(w_out, "tensor", axis=0, tiled=False)

    my_ids = lax.dynamic_slice_in_dim(route_ids, tensor_index * quarter, quarter, 0)
    my_weights = lax.dynamic_slice_in_dim(route_weights, tensor_index * quarter, quarter, 0)
    named = my_ids.T[:, None, :] == jnp.arange(expert_total, dtype=jnp.int32)[None, :, None]
    table = jnp.sum(jnp.where(named, my_weights.T[:, None, :], 0.0), axis=0)

    attn_in = norm_rows(full_rows, attn_gain)
    queries_t = lax.dot_general(
        w_query, attn_in, (((0,), (1,)), ((), ())), preferred_element_type=jnp.float32
    ).astype(jnp.bfloat16)
    key_weight = lax.dynamic_slice_in_dim(key_matrix, shared * HEAD_DIM, HEAD_DIM, 1)
    value_weight = lax.dynamic_slice_in_dim(value_matrix, shared * HEAD_DIM, HEAD_DIM, 1)
    both = jnp.dot(
        attn_in,
        jnp.concatenate([key_weight, value_weight], axis=1),
        preferred_element_type=jnp.float32,
    ).astype(jnp.bfloat16)
    context = attention(
        queries_t,
        both[:, :HEAD_DIM],
        both[:, HEAD_DIM:],
        key_cache,
        cached_value_rows,
        cache_lengths[0],
        new_lengths[0],
        shared,
    )
    my_rows = lax.dynamic_slice_in_dim(full_rows, tensor_index * quarter, quarter, 0)
    return tail(
        context,
        my_rows,
        table,
        moe_gain[None, :],
        whole_out,
        w_gate[0],
        w_up[0],
        w_down[0],
    )


def solution(mesh):
    placed = (
        P("expert", "tensor"),
        P("expert"),
        P("expert"),
        P("expert", None, None),
        P("expert", None, None),
        P(),
        P(None, "tensor"),
        P(),
        P(),
        P("tensor", None),
        P(),
        P("expert", None),
        P("expert", None),
        P("expert", None, "tensor"),
        P("expert", None, "tensor"),
        P("expert", "tensor", None),
    )
    return jax.shard_map(
        local, mesh=mesh, in_specs=placed, out_specs=P("expert", "tensor"), check_vma=False
    )
```
